128 devices in a mesh: fsdp: 32 (over x, z, core), ckpt: 4 (over y).
Axes of the slice: x: 4, y: 4, z: 4, core: 2. Of those that a mesh axis runs over, the one named last changes fastest.
Arguments:
- act_table: bfloat16 [4, 2048, 4096], P('ckpt', 'fsdp'), may hold values from -6 to 6
- token_ids: int32 [4, 2048], P('ckpt'), may hold values from 0 to 2047, each once within a row
- lengths: int32 [4, 8], P('ckpt'), may hold values from 1 to 384, 2048 in all within a row
- grads: bfloat16 [4, 2048, 14336], P('ckpt', 'fsdp'), may hold values from -0.19921875 to 0.19921875
- weights: bfloat16 [4, 32, 1024, 1792], P('ckpt', 'fsdp'), may hold values from -6 to 6
Outputs:
- merged: bfloat16 [32, 1024, 1792], P('fsdp', 'ckpt')
- merge_weight: float32 [32, 1024, 1792], P('fsdp', 'ckpt')
The draws below stay inside these ranges and needn't reach their ends.
Inputs may be any that keep to these rules, and one draw needn't show every extreme that they name: `token_ids`: each checkpoint's row names every row of the activation table once. One checkpoint's lengths sum to 2048, and one of them is exactly 384.
All inputs are finite; a program needn't handle non-finite values.
Results may differ from the reference program's by a relative error of at most 0.001.
Values may be sent and summed in bfloat16 or wider, within the bound.
A program may use at most 128 MiB of HBM per device.

```python
import math
import jax
import jax.numpy as jnp
import numpy as np
from jax import lax

D = 4096
FFW = 14336
NCB = 8
EX = 8
CKPTS = 4
NFB = 4
TILES = 32
TOK = 2048
MOST = 384
N_CKPT = 4


def levels(stream_key, extent, pieces, low, top_value):
    level = 1.0
    for dim, blocks in pieces:
        heights = jax.random.uniform(jax.random.fold_in(jax.random.fold_in(stream_key, 6), dim), (blocks,), jnp.float32, low / len(pieces), top_value / len(pieces))
        level = level * jnp.repeat(jnp.exp(heights), extent[dim] // blocks).reshape((-1,) + (1,) * (len(extent) - 1 - dim))
    return level


def split_up(number_of, total, reach, slope):
    weights = [(1 << 20) // math.isqrt(standing ** slope) + 1 for standing in range(2, number_of + 1)]
    rest, holding = total - reach - (number_of - 1), [1] * (number_of - 1)
    while rest > 0:
        movable = [i for i in range(number_of - 1) if holding[i] < reach]
        pool, remaining = sum([weights[i] for i in movable]), rest
        for i in movable:
            addition = min(reach - holding[i], max(1, remaining * weights[i] // pool), rest)
            holding[i] = holding[i] + addition
            rest = rest - addition
    return np.array([reach] + holding)


def ragged_sizes(own_key, number_of, total, most, lean):
    if number_of == 2:
        one = jax.random.randint(own_key, (), max(1, total - most), min(most, total - 1) + 1)
        return jnp.stack([one, total - one])
    sizes = jnp.asarray(split_up(number_of, total, most, lean), jnp.int32)
    twos = (number_of - 1) // 2
    giver, sink = sizes[1:1 + 2 * twos:2], sizes[2:2 + 2 * twos:2]
    margin = jnp.minimum(giver - 1, most - sink)
    shifted = jax.random.randint(jax.random.fold_in(own_key, 1), (twos,), 0, 1 << 20) % (margin + 1)
    sizes = sizes.at[1:1 + 2 * twos:2].set(giver - shifted).at[2:2 + 2 * twos:2].set(sink + shifted)
    return sizes[jax.random.permutation(jax.random.fold_in(own_key, 2), number_of)]


def bell_draw(stream_key, dims, deviation, reach, cuts=(), kind=jnp.bfloat16):
    level = levels(stream_key, dims, cuts, -0.22, 0.18) if cuts else 1.0
    result = jax.random.normal(stream_key, dims, jnp.float32) * deviation * level
    return jnp.minimum(jnp.maximum(result, -reach), reach).astype(kind)


def setup_inputs(seed: int = 0) -> dict:
    seeds = jax.random.split(jax.random.key(seed), 6)
    return {
        "act_table": bell_draw(seeds[0], (CKPTS, TOK, D), 1.0, 6.0, ((0, 4), (1, 32))),
        "token_ids": jax.vmap(lambda own: jax.random.permutation(own, TOK))(jax.random.split(seeds[1], CKPTS)).reshape((CKPTS, TOK)).astype(jnp.int32),
        "lengths": jax.vmap(lambda own: ragged_sizes(own, EX, TOK, MOST, 1))(jax.random.split(seeds[2], CKPTS)).reshape((CKPTS, EX)).astype(jnp.int32),
        "grads": bell_draw(seeds[3], (CKPTS, TOK, FFW), 0.03, 0.19921875, ((0, 4), (1, 32))),
        "weights": bell_draw(seeds[4], (CKPTS, TILES, D // NFB, FFW // NCB), 1.0, 6.0, ((0, 4), (1, 32))),
    }


prior_mass = 0.1


def example_fisher(act_rows, grad_rows, example_lengths):
    row_starts = (jnp.cumsum(example_lengths) - example_lengths).astype(jnp.int32)
    padded_rows = jnp.concatenate([act_rows, jnp.zeros((MOST, act_rows.shape[1]), act_rows.dtype)], 0)
    padded_grads = jnp.concatenate([grad_rows, jnp.zeros((MOST, grad_rows.shape[1]), grad_rows.dtype)], 0)
    positions = jnp.arange(MOST, dtype=jnp.int32)

    def add_example(example, running):
        row_start = row_starts[example].astype(jnp.int32)
        act_block = lax.dynamic_slice_in_dim(padded_rows, row_start, MOST, 0)
        keep = (positions < example_lengths[example])[:, None]
        act_block = jnp.where(keep, act_block, jnp.zeros_like(act_block))
        grad_block = lax.dynamic_slice_in_dim(padded_grads, row_start, MOST, 0)
        example_grad = lax.dot_general(act_block, grad_block, (((0,), (0,)), ((), ())), preferred_element_type=jnp.float32)
        return running + example_grad * example_grad

    start_value = jnp.zeros((act_rows.shape[1], grad_rows.shape[1]), jnp.float32)
    return lax.fori_loop(0, example_lengths.shape[0], add_example, start_value)


def to_tiles(full):
    blocked = full.reshape(NFB, D // NFB, NCB, FFW // NCB)
    return jnp.transpose(blocked, (0, 2, 1, 3)).reshape(NFB * NCB, D // NFB, FFW // NCB)


def reference(act_table, token_ids, lengths, grads, weights):
    numerator = jnp.zeros((TILES, D // NFB, FFW // NCB), jnp.float32)
    denominator = jnp.zeros((TILES, D // NFB, FFW // NCB), jnp.float32)
    for member in range(N_CKPT):
        act_rows = act_table[member][token_ids[member]]
        fisher = to_tiles(example_fisher(act_rows, grads[member], lengths[member]))
        fisher_mass = fisher + prior_mass
        numerator = numerator + fisher_mass * weights[member].astype(jnp.float32)
        denominator = denominator + fisher_mass
    return (numerator / denominator).astype(jnp.bfloat16), denominator / N_CKPT
```

```python
import jax
import jax.numpy as jnp
from jax import lax
from jax.experimental import pallas as pl
from jax.experimental.pallas import tpu as pltpu
from jax.sharding import PartitionSpec as P

PRIOR = 0.1
ROWS = 512
SPANS = (
    (0, 384), (0, 768), (0, 1152), (128, 1536), (512, 1920), (896, 2048), (1280, 2048), (1664, 2048),
)
CHUNKS = (256,) * 7
LOW, HIGH = -3.32195, 20.04
LN2 = 0.6931471805599453
SCALE = 65535.0 / (HIGH - LOW)
MESH = pl.DeviceIdType.MESH


def kernel(
    act, ids, lengths, grads, weights, merged, mean_mass,
    piece, rows_t, act_t, windows, fisher, own_w, got_w, own_mass, sent, got, blocks,
    a_send, a_recv, g_send, g_recv, z_send, z_recv, x_send, x_recv, w_send, w_recv, m_send, m_recv, own_sem,
):
    me = lax.axis_index("fsdp")
    y = lax.axis_index("ckpt")
    x, zc = me // 8, me % 8
    z, c = zc // 2, zc % 2
    up, down = (z + 1) % 4, (z + 3) % 4
    right, left = (x + 1) % 4, (x + 3) % 4
    offsets = [sum(CHUNKS[:j]) for j in range(len(CHUNKS))]
    n = len(CHUNKS)
    width = sum(CHUNKS)

    def plane(index):
        return {"fsdp": index, "ckpt": y}

    def column(index):
        return {"fsdp": me, "ckpt": index}

    barrier = pltpu.get_barrier_semaphore()

    @pl.loop(1, 32)
    def _(k):
        pl.semaphore_signal(barrier, inc=1, device_id=plane((me + k) % 32), device_id_type=MESH)

    for d in range(1, 4):
        pl.semaphore_signal(barrier, inc=1, device_id=column((y + d) % 4), device_id_type=MESH)
    pl.semaphore_wait(barrier, 34)

    def remote(src, dst, send, recv, target):
        return pltpu.make_async_remote_copy(
            src_ref=src, dst_ref=dst, send_sem=send, recv_sem=recv, device_id=target, device_id_type=MESH
        )

    def sized(ref, sem):
        pltpu.make_async_copy(ref, ref, sem).wait()

    def z_start(j):
        wide = CHUNKS[j]
        dst = blocks[j].at[pl.ds(pl.multiple_of(me * 64, 64), 64)]

        def src(block):
            return grads.at[0, :, pl.ds(pl.multiple_of(block * width + offsets[j], 128), wide)]

        @pl.loop(1, 8)
        def _(k):
            other = (zc + k) % 8
            remote(src(other), dst, z_send.at[j], z_recv.at[j], plane(x * 8 + other)).start()

        pltpu.make_async_copy(src(zc), dst, z_recv.at[j]).start()

    def band(j, which, first=0, count=512):
        return blocks[j].at[pl.ds(pl.multiple_of(which * 512 + first, 64), count)]

    x_targets = {0: right, 1: left, 2: right, 3: left}

    def x_copy(j, i):
        part = (band(j, x), band(j, x), band(j, left, 0, 256), band(j, right, 256, 256))[i]
        return remote(part, part, x_send.at[j, i], x_recv.at[j, i], plane(x_targets[i] * 8 + zc))

    def x_arrived(j, i):
        part = (band(j, left), band(j, right), band(j, (x + 2) % 4, 0, 256), band(j, (x + 2) % 4, 256, 256))[i]
        sized(part, x_recv.at[j, i])

    def x_start(j):
        sized(band(j, x), z_recv.at[j])
        x_copy(j, 0).start()
        x_copy(j, 1).start()

    def x_pass(j):
        x_arrived(j, 0)
        x_copy(j, 2).start()
        x_arrived(j, 1)
        x_copy(j, 3).start()

    def x_finish(j):
        x_arrived(j, 2)
        x_arrived(j, 3)

    def a_source(target):
        return act.at[0, :, pl.ds(pl.multiple_of(target * 128, 128), 128)]

    z_start(0)
    a_rows = piece.at[pl.ds(pl.multiple_of(me * 64, 64), 64)]

    @pl.loop(1, 32)
    def _(k):
        target = (me + k) % 32
        remote(a_source(target), a_rows, a_send, a_recv, plane(target)).start()

    pltpu.make_async_copy(a_source(me), a_rows, a_recv).start()

    def w_rows(owner):
        return weights.at[0, 0, pl.ds(pl.multiple_of(owner * 256, 256), 256)]

    w_copies = [
        remote(w_rows((y + d) % 4), got_w.at[d - 1], w_send.at[d - 1], w_recv.at[d - 1], column((y + d) % 4))
        for d in range(1, 4)
    ]
    z_start(1)
    for copy in w_copies:
        copy.start()
    own_copy = pltpu.make_async_copy(w_rows(y), own_w, own_sem)
    own_copy.start()
    for j in range(2, n):
        z_start(j)

    first_of = [jnp.int32(0)]
    for e in range(8):
        first_of.append(first_of[e] + lengths[0, e])

    x_start(0)
    sized(piece, a_recv)

    @pl.loop(0, 8)
    def _(b):
        at = pl.ds(pl.multiple_of(b * 256, 256), 256)
        rows_t[:, at] = piece[at, :].astype(jnp.float32).T.astype(jnp.bfloat16)

    x_start(1)

    @pl.loop(0, 8)
    def _(b):
        at = pl.ds(pl.multiple_of(b * 256, 256), 256)
        hot = lax.broadcasted_iota(jnp.int32, (2048, 256), 0) == ids[:, at]
        hot = jnp.where(hot, jnp.float32(1), jnp.float32(0)).astype(jnp.bfloat16)
        placed = jnp.dot(rows_t[...], hot, preferred_element_type=jnp.float32)
        act_t[zc, :, at] = placed.astype(jnp.bfloat16)

    other_core = plane(x * 8 + z * 2 + 1 - c)

    def g_copy(i):
        own, below, above, far = (
            act_t.at[zc], act_t.at[down * 2 + c], act_t.at[up * 2 + c], act_t.at[((z + 2) % 4) * 2 + c],
        )
        part, target = (
            (own, plane(x * 8 + up * 2 + c)),
            (own, plane(x * 8 + down * 2 + c)),
            (below.at[pl.ds(0, 64)], plane(x * 8 + up * 2 + c)),
            (above.at[pl.ds(64, 64)], plane(x * 8 + down * 2 + c)),
            (own, other_core),
            (below, other_core),
            (above, other_core),
            (far, other_core),
        )[i]
        return remote(part, part, g_send.at[i], g_recv.at[i], target)

    def g_arrived(i):
        o = 1 - c
        far = act_t.at[((z + 2) % 4) * 2 + c]
        part = (
            act_t.at[down * 2 + c], act_t.at[up * 2 + c], far.at[pl.ds(0, 64)], far.at[pl.ds(64, 64)],
            act_t.at[z * 2 + o], act_t.at[down * 2 + o], act_t.at[up * 2 + o], act_t.at[((z + 2) % 4) * 2 + o],
        )[i]
        sized(part, g_recv.at[i])

    for i in (0, 1, 4):
        g_copy(i).start()
    x_pass(0)
    x_start(2)
    g_arrived(0)
    g_copy(2).start()
    g_copy(5).start()
    g_arrived(1)
    g_copy(3).start()
    g_copy(6).start()
    x_pass(1)
    g_arrived(2)
    g_arrived(3)
    g_copy(7).start()
    x_start(3)
    for i in (4, 5, 6, 7):
        g_arrived(i)

    for e, (low, high) in enumerate(SPANS):
        position = low + lax.broadcasted_iota(jnp.int32, (1, high - low), 1)
        keep = (position >= first_of[e]) & (position < first_of[e] + lengths[0, e])
        keep = jnp.where(keep, jnp.float32(1), jnp.float32(0)).astype(jnp.bfloat16)

        @pl.loop(0, 8)
        def _(q):
            windows[e][pl.ds(pl.multiple_of(q * 128, 128), 128), :] = act_t[q, :, low:high] * keep

    def compute(j):
        wide = CHUNKS[j]

        @pl.loop(0, 1024 // ROWS)
        def _(q):
            at = pl.ds(pl.multiple_of(q * ROWS, ROWS), ROWS)
            for e, (low, high) in enumerate(SPANS):
                part = jnp.dot(windows[e][at, :], blocks[j][low:high, :], preferred_element_type=jnp.float32)
                part = part * part
                fisher[at, :wide] = part + (PRIOR if e == 0 else fisher[at, :wide])

        @pl.loop(0, 4)
        def _(q):
            at = pl.ds(pl.multiple_of(q * 256, 256), 256)
            code = jnp.log(fisher[at, :wide]) * (SCALE / LN2) - (LOW * SCALE + 32767.5)
            code = jnp.clip(jnp.floor(code), -32768.0, 32767.0).astype(jnp.int32)
            sent[j][at, :] = code.astype(jnp.int16)

        own_mass[:, offsets[j] : offsets[j] + wide] = fisher[pl.ds(pl.multiple_of(y * 256, 256), 256), :wide]

    def m_copy(j, d):
        owner = (y + d) % 4
        return remote(
            sent[j].at[pl.ds(pl.multiple_of(owner * 256, 256), 256)],
            got[j].at[d - 1], m_send.at[j, d - 1], m_recv.at[j, d - 1], column(owner),
        )

    def combine(j):
        columns = slice(offsets[j], offsets[j] + CHUNKS[j])
        for d in range(1, 4):
            sized(got[j].at[d - 1], m_recv.at[j, d - 1])

        @pl.loop(0, 8)
        def _(q):
            at = pl.ds(pl.multiple_of(q * 32, 32), 32)
            total = own_mass[at, columns]
            weighted = total * own_w[at, columns].astype(jnp.float32)
            for d in range(3):
                code = got[j][d, at, :].astype(jnp.int32).astype(jnp.float32)
                mass = jnp.exp((code + (32768.0 + LOW * SCALE)) * (LN2 / SCALE))
                total += mass
                weighted += mass * got_w[d, at, columns].astype(jnp.float32)
            merged[0, at, columns] = (weighted / total).astype(jnp.bfloat16)
            mean_mass[0, at, columns] = total * 0.25

    for j in range(n):
        if j + 1 < n and j > 0:
            x_pass(j + 1)
        if j + 3 < n and j > 0:
            x_start(j + 3)
        x_finish(j)
        compute(j)
        for d in range(1, 4):
            m_copy(j, d).start()
        if j == 0:
            own_copy.wait()
            for i in range(3):
                sized(got_w.at[i], w_recv.at[i])
        if j >= 2:
            combine(j - 2)
    combine(n - 2)
    combine(n - 1)

    pltpu.make_async_copy(piece.at[pl.ds(0, 31 * 64)], piece.at[pl.ds(0, 31 * 64)], a_send).wait()
    for copy in w_copies:
        copy.wait_send()
    for i in range(8):
        g_copy(i).wait_send()
    for j in range(n):
        sized(blocks[j].at[pl.ds(0, 7 * 64)], z_send.at[j])
        for i in range(4):
            x_copy(j, i).wait_send()
        for d in range(1, 4):
            m_copy(j, d).wait_send()


def body(act_table, token_ids, lengths, grads, weights):
    n = len(CHUNKS)
    wide = sum(CHUNKS)
    dma = pltpu.SemaphoreType.DMA
    whole = pl.BlockSpec(memory_space=pltpu.VMEM)
    anywhere = pl.BlockSpec(memory_space=pl.ANY)
    return pl.pallas_call(
        kernel,
        out_shape=(
            jax.ShapeDtypeStruct((1, 256, wide), jnp.bfloat16),
            jax.ShapeDtypeStruct((1, 256, wide), jnp.float32),
        ),
        in_specs=[anywhere, whole, pl.BlockSpec(memory_space=pltpu.SMEM), anywhere, anywhere],
        out_specs=(whole, whole),
        scratch_shapes=[
            pltpu.VMEM((2048, 128), jnp.bfloat16),
            pltpu.VMEM((128, 2048), jnp.bfloat16),
            pltpu.VMEM((8, 128, 2048), jnp.bfloat16),
            tuple(pltpu.VMEM((1024, high - low), jnp.bfloat16) for low, high in SPANS),
            pltpu.VMEM((1024, max(CHUNKS)), jnp.float32),
            pltpu.VMEM((256, wide), jnp.bfloat16),
            pltpu.VMEM((3, 256, wide), jnp.bfloat16),
            pltpu.VMEM((256, wide), jnp.float32),
            tuple(pltpu.VMEM((1024, w), jnp.int16) for w in CHUNKS),
            tuple(pltpu.VMEM((3, 256, w), jnp.int16) for w in CHUNKS),
            tuple(pltpu.VMEM((2048, w), jnp.bfloat16) for w in CHUNKS),
            dma, dma, dma((8,)), dma((8,)), dma((n,)), dma((n,)), dma((n, 4)), dma((n, 4)),
            dma((3,)), dma((3,)), dma((n, 3)), dma((n, 3)), dma,
        ],
        compiler_params=pltpu.CompilerParams(
            collective_id=0, has_side_effects=True, vmem_limit_bytes=58 << 20
        ),
    )(act_table, token_ids, lengths, grads, weights)


def solution(mesh):
    placed = (
        P("ckpt", "fsdp", None),
        P("ckpt", None),
        P("ckpt", None),
        P("ckpt", "fsdp", None),
        P("ckpt", "fsdp", None, None),
    )
    return jax.shard_map(
        body,
        mesh=mesh,
        in_specs=placed,
        out_specs=(P("fsdp", "ckpt", None), P("fsdp", "ckpt", None)),
        check_vma=False,
    )
```

```python
import jax
import jax.numpy as jnp
from jax import lax
from jax.experimental import pallas as pl
from jax.experimental.pallas import tpu as pltpu
from jax.sharding import PartitionSpec as P

PRIOR = 0.1
CHUNKS = (256,) * 6 + (128,) * 2
LOW, HIGH = -3.32195, 20.04
LN2 = 0.6931471805599453
SCALE = 65535.0 / (HIGH - LOW)
MESH = pl.DeviceIdType.MESH
ORDER = (
    "A", "z0", "W", "z1", "H", "z2", "s0", "s1", "T", "P", "G", "z3", "s2", "p0", "X", "B", "U", "z4",
    "s3", "p1", "F", "z5", "Y", "Z", "s4", "p2", "z6", "z7", "f0", "c0", "p3", "s5", "f1", "c1", "p4",
    "s6", "f2", "c2", "V", "o0", "p5", "s7", "f3", "c3", "o1", "p6", "f4", "c4", "o2", "p7", "f5", "c5",
    "o3", "f6", "c6", "o4", "f7", "c7", "o5", "o6", "o7",
)


def kernel(
    act, ids, lengths, grads, weights, merged, mean_mass,
    piece, rows_t, act_t, windows, framed, fisher, own_w, got_w, own_mass, sent, got, blocks,
    a_send, a_recv, g_send, g_recv, z_send, z_recv, x_send, x_recv, w_send, w_recv, m_send, m_recv, own_sem,
):
    me = lax.axis_index("fsdp")
    y = lax.axis_index("ckpt")
    x, zc = me // 8, me % 8
    z, c = zc // 2, zc % 2
    up, down = (z + 1) % 4, (z + 3) % 4
    right, left = (x + 1) % 4, (x + 3) % 4
    offsets = [sum(CHUNKS[:j]) for j in range(len(CHUNKS))]
    n = len(CHUNKS)
    width = sum(CHUNKS)

    def plane(index):
        return {"fsdp": index, "ckpt": y}

    def column(index):
        return {"fsdp": me, "ckpt": index}

    barrier = pltpu.get_barrier_semaphore()

    @pl.loop(1, 32)
    def _(k):
        pl.semaphore_signal(barrier, inc=1, device_id=plane((me + k) % 32), device_id_type=MESH)

    for d in range(1, 4):
        pl.semaphore_signal(barrier, inc=1, device_id=column((y + d) % 4), device_id_type=MESH)
    pl.semaphore_wait(barrier, 34)

    def remote(src, dst, send, recv, target):
        return pltpu.make_async_remote_copy(
            src_ref=src, dst_ref=dst, send_sem=send, recv_sem=recv, device_id=target, device_id_type=MESH
        )

    def sized(ref, sem):
        pltpu.make_async_copy(ref, ref, sem).wait()

    def z_start(j):
        wide = CHUNKS[j]
        dst = blocks[j].at[me // 2, pl.ds(pl.multiple_of((me % 2) * 64, 64), 64)]

        def src(block):
            return grads.at[0, :, pl.ds(pl.multiple_of(block * width + offsets[j], 128), wide)]

        @pl.loop(1, 8)
        def _(k):
            other = (zc + k) % 8
            remote(src(other), dst, z_send.at[j], z_recv.at[j], plane(x * 8 + other)).start()

        pltpu.make_async_copy(src(zc), dst, z_recv.at[j]).start()

    def band(j, which, first=0, count=4):
        return blocks[j].at[pl.ds(which * 4 + first, count)]

    x_targets = {0: right, 1: left, 2: right, 3: left}

    def x_copy(j, i):
        part = (band(j, x), band(j, x), band(j, left, 0, 2), band(j, right, 2, 2))[i]
        return remote(part, part, x_send.at[j, i], x_recv.at[j, i], plane(x_targets[i] * 8 + zc))

    def x_arrived(j, i):
        part = (band(j, left), band(j, right), band(j, (x + 2) % 4, 0, 2), band(j, (x + 2) % 4, 2, 2))[i]
        sized(part, x_recv.at[j, i])

    def x_start(j):
        sized(band(j, x), z_recv.at[j])
        x_copy(j, 0).start()
        x_copy(j, 1).start()

    def x_pass(j):
        x_arrived(j, 0)
        x_copy(j, 2).start()
        x_arrived(j, 1)
        x_copy(j, 3).start()

    def x_finish(j):
        x_arrived(j, 2)
        x_arrived(j, 3)

    def a_source(target):
        return act.at[0, :, pl.ds(pl.multiple_of(target * 128, 128), 128)]

    a_rows = piece.at[pl.ds(pl.multiple_of(me * 64, 64), 64)]

    def a_start():
        @pl.loop(1, 32)
        def _(k):
            target = (me + k) % 32
            remote(a_source(target), a_rows, a_send, a_recv, plane(target)).start()

        pltpu.make_async_copy(a_source(me), a_rows, a_recv).start()

    def w_rows(owner):
        return weights.at[0, 0, pl.ds(pl.multiple_of(owner * 256, 256), 256)]

    w_copies = [
        remote(w_rows((y + d) % 4), got_w.at[d - 1], w_send.at[d - 1], w_recv.at[d - 1], column((y + d) % 4))
        for d in range(1, 4)
    ]
    own_copy = pltpu.make_async_copy(w_rows(y), own_w, own_sem)

    def w_start():
        for copy in w_copies:
            copy.start()
        own_copy.start()

    def w_arrived():
        own_copy.wait()
        for i in range(3):
            sized(got_w.at[i], w_recv.at[i])

    first_of = [jnp.int32(0)]
    for e in range(8):
        first_of.append(first_of[e] + lengths[0, e])

    lead, keeps = [], []
    for e in range(8):
        lead.append(jnp.minimum(first_of[e] // 128, 12))
        position = lead[e] * 128 + lax.broadcasted_iota(jnp.int32, (1, 512), 1)
        keep = (position >= first_of[e]) & (position < first_of[e] + lengths[0, e])
        keeps.append(jnp.where(keep, jnp.float32(1), jnp.float32(0)).astype(jnp.bfloat16))

    def a_turn():
        sized(piece, a_recv)

        @pl.loop(0, 8)
        def _(b):
            at = pl.ds(pl.multiple_of(b * 256, 256), 256)
            rows_t[:, at] = piece[at, :].astype(jnp.float32).T.astype(jnp.bfloat16)

    def hot_build():
        @pl.loop(0, 8)
        def _(b):
            own = ids[:, pl.ds(pl.multiple_of(b * 256, 256), 256)]
            for h in range(2):
                hot = lax.broadcasted_iota(jnp.int32, (1024, 256), 0) + h * 1024 == own
                hot = jnp.where(hot, jnp.float32(1), jnp.float32(0)).astype(jnp.bfloat16)
                windows[b, :, h * 256 : (h + 1) * 256] = hot

    def a_permute():
        @pl.loop(0, 8)
        def _(b):
            placed = sum(
                jnp.dot(
                    rows_t[:, h * 1024 : (h + 1) * 1024],
                    windows[b, :, h * 256 : (h + 1) * 256],
                    preferred_element_type=jnp.float32,
                )
                for h in range(2)
            )
            for i in range(2):
                act_t[0][b * 2 + i] = placed[:, i * 128 : (i + 1) * 128].astype(jnp.bfloat16)

    above_core, below_core = plane(x * 8 + up * 2 + c), plane(x * 8 + down * 2 + c)
    other_core = plane(x * 8 + z * 2 + 1 - c)
    first_half, second_half = pl.ds(0, 8), pl.ds(8, 8)

    def g_copy(i):
        src, dst, target = (
            (act_t[0], act_t[1], above_core),
            (act_t[0], act_t[2], below_core),
            (act_t[1].at[first_half], act_t[3].at[first_half], above_core),
            (act_t[2].at[second_half], act_t[3].at[second_half], below_core),
            (act_t[0], act_t[4], other_core),
            (act_t[1], act_t[5], other_core),
            (act_t[2], act_t[6], other_core),
            (act_t[3], act_t[7], other_core),
        )[i]
        return remote(src, dst, g_send.at[i], g_recv.at[i], target)

    def g_arrived(i):
        part = (
            act_t[1], act_t[2], act_t[3].at[first_half], act_t[3].at[second_half],
            act_t[4], act_t[5], act_t[6], act_t[7],
        )[i]
        sized(part, g_recv.at[i])

    def mask(k):
        owner = (z + (0, 3, 1, 2)[k % 4]) % 4 * 2 + (c if k < 4 else 1 - c)
        for e in range(8):
            for i in range(4):
                at = slice(i * 128, (i + 1) * 128)
                rows = pl.ds(pl.multiple_of(owner * 128, 128), 128)
                windows[e, rows, at] = act_t[k][lead[e] + i] * keeps[e][:, at]

    def g_start():
        for i in (0, 1, 4):
            g_copy(i).start()

    def g_below():
        g_arrived(0)
        g_copy(2).start()
        g_copy(5).start()

    def g_above():
        g_arrived(1)
        g_copy(3).start()
        g_copy(6).start()

    def g_far():
        g_arrived(2)
        g_arrived(3)
        g_copy(7).start()

    def mask_own():
        mask(0)
        g_arrived(4)
        mask(4)

    def mask_near():
        mask(1)
        mask(2)
        g_arrived(5)
        mask(5)
        g_arrived(6)
        mask(6)

    def mask_far():
        mask(3)
        g_arrived(7)
        mask(7)

    def m_copy(j, d):
        owner = (y + d) % 4
        return remote(
            sent[j].at[pl.ds(pl.multiple_of(owner * 256, 256), 256)],
            got[j].at[d - 1], m_send.at[j, d - 1], m_recv.at[j, d - 1], column(owner),
        )

    def rows_of(j, owner):
        wide = CHUNKS[j]
        at = pl.ds(pl.multiple_of(owner * 256, 256), 256)
        for e in range(8):
            part = jnp.dot(windows[e, at, :], framed[e, :, :wide], preferred_element_type=jnp.float32)
            part = part * part
            fisher[:, :wide] = part + (PRIOR if e == 0 else fisher[:, :wide])

        @pl.when(owner != y)
        def _():
            code = jnp.log(fisher[:, :wide]) * (SCALE / LN2) - (LOW * SCALE + 32767.5)
            code = jnp.clip(jnp.floor(code), -32768.0, 32767.0).astype(jnp.int32)
            sent[j][at, :] = code.astype(jnp.int16)
            m_copy(j, (owner + 4 - y) % 4).start()

        @pl.when(owner == y)
        def _():
            own_mass[:, offsets[j] : offsets[j] + wide] = fisher[:, :wide]

    def frame(j):
        for e in range(8):
            for i in range(4):
                framed[e, i * 128 : (i + 1) * 128, : CHUNKS[j]] = blocks[j][lead[e] + i]

    def compute(j):
        frame(j)

        @pl.loop(0, 4)
        def _(t):
            rows_of(j, (y + ((t + 1) % 3 + 1) * (1 - t // 3)) % 4)

    def combine(j):
        columns = slice(offsets[j], offsets[j] + CHUNKS[j])
        for d in range(1, 4):
            sized(got[j].at[d - 1], m_recv.at[j, d - 1])

        @pl.loop(0, 8)
        def _(q):
            at = pl.ds(pl.multiple_of(q * 32, 32), 32)
            total = own_mass[at, columns]
            weighted = total * own_w[at, columns].astype(jnp.float32)
            for d in range(3):
                code = got[j][d, at, :].astype(jnp.int32).astype(jnp.float32)
                mass = jnp.exp((code + (32768.0 + LOW * SCALE)) * (LN2 / SCALE))
                total += mass
                weighted += mass * got_w[d, at, columns].astype(jnp.float32)
            merged[0, at, columns] = (weighted / total).astype(jnp.bfloat16)
            mean_mass[0, at, columns] = total * 0.25

    steps = {
        "z": z_start, "s": x_start, "p": x_pass, "f": x_finish, "c": compute, "o": combine,
        "A": a_start, "W": w_start, "V": w_arrived, "T": a_turn, "H": hot_build, "P": a_permute, "G": g_start, "B": g_below,
        "U": g_above, "F": g_far, "X": mask_own, "Y": mask_near, "Z": mask_far,
    }
    for step in ORDER:
        steps[step[0]](*(int(j) for j in step[1:]))

    pltpu.make_async_copy(piece.at[pl.ds(0, 31 * 64)], piece.at[pl.ds(0, 31 * 64)], a_send).wait()
    for copy in w_copies:
        copy.wait_send()
    for i in range(8):
        g_copy(i).wait_send()
    for j in range(n):
        sized(blocks[j].at[pl.ds(0, 7), pl.ds(0, 64)], z_send.at[j])
        for i in range(4):
            x_copy(j, i).wait_send()
        for d in range(1, 4):
            m_copy(j, d).wait_send()


def body(act_table, token_ids, lengths, grads, weights):
    n = len(CHUNKS)
    wide = sum(CHUNKS)
    dma = pltpu.SemaphoreType.DMA
    whole = pl.BlockSpec(memory_space=pltpu.VMEM)
    anywhere = pl.BlockSpec(memory_space=pl.ANY)
    return pl.pallas_call(
        kernel,
        out_shape=(
            jax.ShapeDtypeStruct((1, 256, wide), jnp.bfloat16),
            jax.ShapeDtypeStruct((1, 256, wide), jnp.float32),
        ),
        in_specs=[anywhere, whole, pl.BlockSpec(memory_space=pltpu.SMEM), anywhere, anywhere],
        out_specs=(whole, whole),
        scratch_shapes=[
            pltpu.VMEM((2048, 128), jnp.bfloat16),
            pltpu.VMEM((128, 2048), jnp.bfloat16),
            tuple(pltpu.VMEM((16, 128, 128), jnp.bfloat16) for _ in range(8)),
            pltpu.VMEM((8, 1024, 512), jnp.bfloat16),
            pltpu.VMEM((8, 512, max(CHUNKS)), jnp.bfloat16),
            pltpu.VMEM((256, max(CHUNKS)), jnp.float32),
            pltpu.VMEM((256, wide), jnp.bfloat16),
            pltpu.VMEM((3, 256, wide), jnp.bfloat16),
            pltpu.VMEM((256, wide), jnp.float32),
            tuple(pltpu.VMEM((1024, w), jnp.int16) for w in CHUNKS),
            tuple(pltpu.VMEM((3, 256, w), jnp.int16) for w in CHUNKS),
            tuple(pltpu.VMEM((16, 128, w), jnp.bfloat16) for w in CHUNKS),
            dma, dma, dma((8,)), dma((8,)), dma((n,)), dma((n,)), dma((n, 4)), dma((n, 4)),
            dma((3,)), dma((3,)), dma((n, 3)), dma((n, 3)), dma,
        ],
        compiler_params=pltpu.CompilerParams(
            collective_id=0, has_side_effects=True, vmem_limit_bytes=50 << 20
        ),
    )(act_table, token_ids, lengths, grads, weights)


def solution(mesh):
    placed = (
        P("ckpt", "fsdp", None),
        P("ckpt", None),
        P("ckpt", None),
        P("ckpt", "fsdp", None),
        P("ckpt", "fsdp", None, None),
    )
    return jax.shard_map(
        body,
        mesh=mesh,
        in_specs=placed,
        out_specs=(P("fsdp", "ckpt", None), P("fsdp", "ckpt", None)),
        check_vma=False,
    )
```

```python
import jax
import jax.numpy as jnp
from jax import lax
from jax.experimental import pallas as pl
from jax.experimental.pallas import tpu as pltpu
from jax.sharding import PartitionSpec as P

PRIOR = 0.1
CHUNKS = (256,) * 6 + (128,) * 2
LOW, HIGH = -3.32195, 20.04
LN2 = 0.6931471805599453
SCALE = 65535.0 / (HIGH - LOW)
MESH = pl.DeviceIdType.MESH
ORDER = (
    "A", "z0", "W", "z1", "H", "z2", "s0", "s1", "T", "P", "G", "z3", "s2", "p0", "X", "B", "U", "z4",
    "s3", "p1", "F", "z5", "Y", "Z", "s4", "p2", "z6", "z7", "f0", "c0", "p3", "s5", "f1", "c1", "p4",
    "s6", "f2", "c2", "V", "o0", "p5", "s7", "f3", "c3", "o1", "p6", "f4", "c4", "o2", "p7", "f5", "c5",
    "o3", "f6", "c6", "o4", "f7", "c7", "o5", "o6", "o7",
)


def kernel(
    act, ids, lengths, grads, weights, merged, mean_mass,
    piece, rows_t, act_t, windows, framed, fisher, own_w, got_w, own_mass, sent, got, blocks,
    a_send, a_recv, g_send, g_recv, z_send, z_recv, x_send, x_recv, w_send, w_recv, m_send, m_recv, own_sem,
):
    me = lax.axis_index("fsdp")
    y = lax.axis_index("ckpt")
    x, zc = me // 8, me % 8
    z, c = zc // 2, zc % 2
    up, down = (z + 1) % 4, (z + 3) % 4
    right, left = (x + 1) % 4, (x + 3) % 4
    offsets = [sum(CHUNKS[:j]) for j in range(len(CHUNKS))]
    n = len(CHUNKS)
    width = sum(CHUNKS)

    def plane(index):
        return {"fsdp": index, "ckpt": y}

    def column(index):
        return {"fsdp": me, "ckpt": index}

    barrier = pltpu.get_barrier_semaphore()

    @pl.loop(1, 32)
    def _(k):
        pl.semaphore_signal(barrier, inc=1, device_id=plane((me + k) % 32), device_id_type=MESH)

    for d in range(1, 4):
        pl.semaphore_signal(barrier, inc=1, device_id=column((y + d) % 4), device_id_type=MESH)
    pl.semaphore_wait(barrier, 34)

    def remote(src, dst, send, recv, target):
        return pltpu.make_async_remote_copy(
            src_ref=src, dst_ref=dst, send_sem=send, recv_sem=recv, device_id=target, device_id_type=MESH
        )

    def sized(ref, sem):
        pltpu.make_async_copy(ref, ref, sem).wait()

    def z_start(j):
        wide = CHUNKS[j]
        dst = blocks[j].at[me // 2, pl.ds(pl.multiple_of((me % 2) * 64, 64), 64)]

        def src(block):
            return grads.at[0, :, pl.ds(pl.multiple_of(block * width + offsets[j], 128), wide)]

        @pl.loop(1, 8)
        def _(k):
            other = (zc + k) % 8
            remote(src(other), dst, z_send.at[j], z_recv.at[j], plane(x * 8 + other)).start()

        pltpu.make_async_copy(src(zc), dst, z_recv.at[j]).start()

    def band(j, which, first=0, count=4):
        return blocks[j].at[pl.ds(which * 4 + first, count)]

    x_targets = {0: right, 1: left, 2: right, 3: left}

    def x_copy(j, i):
        part = (band(j, x), band(j, x), band(j, left, 0, 2), band(j, right, 2, 2))[i]
        return remote(part, part, x_send.at[j, i], x_recv.at[j, i], plane(x_targets[i] * 8 + zc))

    def x_arrived(j, i):
        part = (band(j, left), band(j, right), band(j, (x + 2) % 4, 0, 2), band(j, (x + 2) % 4, 2, 2))[i]
        sized(part, x_recv.at[j, i])

    def x_start(j):
        sized(band(j, x), z_recv.at[j])
        x_copy(j, 0).start()
        x_copy(j, 1).start()

    def x_pass(j):
        x_arrived(j, 0)
        x_copy(j, 2).start()
        x_arrived(j, 1)
        x_copy(j, 3).start()

    def x_finish(j):
        x_arrived(j, 2)
        x_arrived(j, 3)

    def a_source(target):
        return act.at[0, :, pl.ds(pl.multiple_of(target * 128, 128), 128)]

    a_rows = piece.at[pl.ds(pl.multiple_of(me * 64, 64), 64)]

    def a_start():
        @pl.loop(1, 32)
        def _(k):
            target = (me + k) % 32
            remote(a_source(target), a_rows, a_send, a_recv, plane(target)).start()

        pltpu.make_async_copy(a_source(me), a_rows, a_recv).start()

    def w_rows(owner):
        return weights.at[0, 0, pl.ds(pl.multiple_of(owner * 256, 256), 256)]

    w_copies = [
        remote(w_rows((y + d) % 4), got_w.at[d - 1], w_send.at[d - 1], w_recv.at[d - 1], column((y + d) % 4))
        for d in range(1, 4)
    ]
    own_copy = pltpu.make_async_copy(w_rows(y), own_w, own_sem)

    def w_start():
        for copy in w_copies:
            copy.start()
        own_copy.start()

    def w_arrived():
        own_copy.wait()
        for i in range(3):
            sized(got_w.at[i], w_recv.at[i])

    first_of = [jnp.int32(0)]
    for e in range(8):
        first_of.append(first_of[e] + lengths[0, e])

    lead, keeps = [], []
    for e in range(8):
        lead.append(jnp.minimum(first_of[e] // 128, 12))
        position = lead[e] * 128 + lax.broadcasted_iota(jnp.int32, (1, 512), 1)
        keep = (position >= first_of[e]) & (position < first_of[e] + lengths[0, e])
        keeps.append(jnp.where(keep, jnp.float32(1), jnp.float32(0)).astype(jnp.bfloat16))

    def a_turn():
        sized(piece, a_recv)

        @pl.loop(0, 8)
        def _(b):
            at = pl.ds(pl.multiple_of(b * 256, 256), 256)
            rows_t[:, at] = piece[at, :].astype(jnp.float32).T.astype(jnp.bfloat16)

    def hot_build():
        @pl.loop(0, 8)
        def _(b):
            own = ids[:, pl.ds(pl.multiple_of(b * 256, 256), 256)]
            for h in range(2):
                hot = lax.broadcasted_iota(jnp.int32, (1024, 256), 0) + h * 1024 == own
                hot = jnp.where(hot, jnp.float32(1), jnp.float32(0)).astype(jnp.bfloat16)
                windows[b, :, h * 256 : (h + 1) * 256] = hot

    def a_permute():
        @pl.loop(0, 8)
        def _(b):
            placed = sum(
                jnp.dot(
                    rows_t[:, h * 1024 : (h + 1) * 1024],
                    windows[b, :, h * 256 : (h + 1) * 256],
                    preferred_element_type=jnp.float32,
                )
                for h in range(2)
            )
            for i in range(2):
                act_t[0][b * 2 + i] = placed[:, i * 128 : (i + 1) * 128].astype(jnp.bfloat16)

    above_core, below_core = plane(x * 8 + up * 2 + c), plane(x * 8 + down * 2 + c)
    other_core = plane(x * 8 + z * 2 + 1 - c)
    first_half, second_half = pl.ds(0, 8), pl.ds(8, 8)

    def g_copy(i):
        src, dst, target = (
            (act_t[0], act_t[1], above_core),
            (act_t[0], act_t[2], below_core),
            (act_t[1].at[first_half], act_t[3].at[first_half], above_core),
            (act_t[2].at[second_half], act_t[3].at[second_half], below_core),
            (act_t[0], act_t[4], other_core),
            (act_t[1], act_t[5], other_core),
            (act_t[2], act_t[6], other_core),
            (act_t[3], act_t[7], other_core),
        )[i]
        return remote(src, dst, g_send.at[i], g_recv.at[i], target)

    def g_arrived(i):
        part = (
            act_t[1], act_t[2], act_t[3].at[first_half], act_t[3].at[second_half],
            act_t[4], act_t[5], act_t[6], act_t[7],
        )[i]
        sized(part, g_recv.at[i])

    def mask(k):
        owner = (z + (0, 3, 1, 2)[k % 4]) % 4 * 2 + (c if k < 4 else 1 - c)
        for e in range(8):
            for i in range(4):
                at = slice(i * 128, (i + 1) * 128)
                rows = pl.ds(pl.multiple_of(owner * 128, 128), 128)
                windows[e, rows, at] = act_t[k][lead[e] + i] * keeps[e][:, at]

    def g_start():
        for i in (0, 1, 4):
            g_copy(i).start()

    def g_below():
        g_arrived(0)
        g_copy(2).start()
        g_copy(5).start()

    def g_above():
        g_arrived(1)
        g_copy(3).start()
        g_copy(6).start()

    def g_far():
        g_arrived(2)
        g_arrived(3)
        g_copy(7).start()

    def mask_own():
        mask(0)
        g_arrived(4)
        mask(4)

    def mask_near():
        mask(1)
        mask(2)
        g_arrived(5)
        mask(5)
        g_arrived(6)
        mask(6)

    def mask_far():
        mask(3)
        g_arrived(7)
        mask(7)

    def m_copy(j, d):
        owner = (y + d) % 4
        return remote(
            sent[j].at[pl.ds(pl.multiple_of(owner * 256, 256), 256)],
            got[j].at[d - 1], m_send.at[j, d - 1], m_recv.at[j, d - 1], column(owner),
        )

    def rows_of(j, owner):
        wide = CHUNKS[j]
        at = pl.ds(pl.multiple_of(owner * 256, 256), 256)
        for e in range(8):
            part = jnp.dot(windows[e, at, :], framed[e, :, :wide], preferred_element_type=jnp.float32)
            part = part * part
            fisher[:, :wide] = part + (PRIOR if e == 0 else fisher[:, :wide])

        @pl.when(owner != y)
        def _():
            code = jnp.log(fisher[:, :wide]) * (SCALE / LN2) - (LOW * SCALE + 32767.5)
            code = jnp.clip(jnp.floor(code), -32768.0, 32767.0).astype(jnp.int32)
            sent[j][at, :] = code.astype(jnp.int16)
            m_copy(j, (owner + 4 - y) % 4).start()

        @pl.when(owner == y)
        def _():
            own_mass[:, offsets[j] : offsets[j] + wide] = fisher[:, :wide]

    def frame(j):
        for e in range(8):
            for i in range(4):
                framed[e, i * 128 : (i + 1) * 128, : CHUNKS[j]] = blocks[j][lead[e] + i]

    def compute(j):
        frame(j)

        @pl.loop(0, 4)
        def _(t):
            rows_of(j, (y + ((t + 1) % 3 + 1) * (1 - t // 3)) % 4)

    def combine(j):
        columns = slice(offsets[j], offsets[j] + CHUNKS[j])
        for d in range(1, 4):
            sized(got[j].at[d - 1], m_recv.at[j, d - 1])

        @pl.loop(0, 8)
        def _(q):
            at = pl.ds(pl.multiple_of(q * 32, 32), 32)
            total = own_mass[at, columns]
            weighted = total * own_w[at, columns].astype(jnp.float32)
            for d in range(3):
                code = got[j][d, at, :].astype(jnp.int32).astype(jnp.float32)
                mass = jnp.exp((code + (32768.0 + LOW * SCALE)) * (LN2 / SCALE))
                total += mass
                weighted += mass * got_w[d, at, columns].astype(jnp.float32)
            merged[0, at, columns] = (weighted / total).astype(jnp.bfloat16)
            mean_mass[0, at, columns] = total * 0.25

    steps = {
        "z": z_start, "s": x_start, "p": x_pass, "f": x_finish, "c": compute, "o": combine,
        "A": a_start, "W": w_start, "V": w_arrived, "T": a_turn, "H": hot_build, "P": a_permute, "G": g_start, "B": g_below,
        "U": g_above, "F": g_far, "X": mask_own, "Y": mask_near, "Z": mask_far,
    }
    for step in ORDER:
        steps[step[0]](*(int(j) for j in step[1:]))

    pltpu.make_async_copy(piece.at[pl.ds(0, 31 * 64)], piece.at[pl.ds(0, 31 * 64)], a_send).wait()
    for copy in w_copies:
        copy.wait_send()
    for i in range(8):
        g_copy(i).wait_send()
    for j in range(n):
        sized(blocks[j].at[pl.ds(0, 7), pl.ds(0, 64)], z_send.at[j])
        for i in range(4):
            x_copy(j, i).wait_send()
        for d in range(1, 4):
            m_copy(j, d).wait_send()


def body(act_table, token_ids, lengths, grads, weights):
    n = len(CHUNKS)
    wide = sum(CHUNKS)
    dma = pltpu.SemaphoreType.DMA
    whole = pl.BlockSpec(memory_space=pltpu.VMEM)
    anywhere = pl.BlockSpec(memory_space=pl.ANY)
    operands = (act_table, token_ids, lengths, grads, weights)
    operands = [pltpu.with_memory_space_constraint(operand, pltpu.HBM) for operand in operands]
    return pl.pallas_call(
        kernel,
        out_shape=(
            jax.ShapeDtypeStruct((1, 256, wide), jnp.bfloat16),
            jax.ShapeDtypeStruct((1, 256, wide), jnp.float32),
        ),
        in_specs=[anywhere, whole, pl.BlockSpec(memory_space=pltpu.SMEM), anywhere, anywhere],
        out_specs=(whole, whole),
        scratch_shapes=[
            pltpu.VMEM((2048, 128), jnp.bfloat16),
            pltpu.VMEM((128, 2048), jnp.bfloat16),
            tuple(pltpu.VMEM((16, 128, 128), jnp.bfloat16) for _ in range(8)),
            pltpu.VMEM((8, 1024, 512), jnp.bfloat16),
            pltpu.VMEM((8, 512, max(CHUNKS)), jnp.bfloat16),
            pltpu.VMEM((256, max(CHUNKS)), jnp.float32),
            pltpu.VMEM((256, wide), jnp.bfloat16),
            pltpu.VMEM((3, 256, wide), jnp.bfloat16),
            pltpu.VMEM((256, wide), jnp.float32),
            tuple(pltpu.VMEM((1024, w), jnp.int16) for w in CHUNKS),
            tuple(pltpu.VMEM((3, 256, w), jnp.int16) for w in CHUNKS),
            tuple(pltpu.VMEM((16, 128, w), jnp.bfloat16) for w in CHUNKS),
            dma, dma, dma((8,)), dma((8,)), dma((n,)), dma((n,)), dma((n, 4)), dma((n, 4)),
            dma((3,)), dma((3,)), dma((n, 3)), dma((n, 3)), dma,
        ],
        compiler_params=pltpu.CompilerParams(
            collective_id=0, has_side_effects=True, vmem_limit_bytes=50 << 20
        ),
    )(*operands)


def solution(mesh):
    placed = (
        P("ckpt", "fsdp", None),
        P("ckpt", None),
        P("ckpt", None),
        P("ckpt", "fsdp", None),
        P("ckpt", "fsdp", None, None),
    )
    return jax.shard_map(
        body,
        mesh=mesh,
        in_specs=placed,
        out_specs=(P("fsdp", "ckpt", None), P("fsdp", "ckpt", None)),
        check_vma=False,
    )
```

```python
import jax
import jax.numpy as jnp
from jax import lax
from jax.experimental import pallas as pl
from jax.experimental.pallas import tpu as pltpu
from jax.sharding import PartitionSpec as P

PRIOR = 0.1
CHUNKS = (256,) * 6 + (128,) * 2
LOW, HIGH = -3.32195, 20.04
LN2 = 0.6931471805599453
SCALE = 65535.0 / (HIGH - LOW)
MESH = pl.DeviceIdType.MESH
ORDER = (
    "A", "z0", "W", "z1", "H", "z2", "s0", "s1", "T", "P0", "g", "P1", "G", "z3", "s2", "p0", "X", "B", "U", "z4",
    "s3", "p1", "F", "z5", "Y", "Z", "s4", "p2", "z6", "z7", "f0", "c0", "p3", "s5", "f1", "c1", "p4",
    "s6", "f2", "c2", "V", "o0", "p5", "s7", "f3", "c3", "o1", "p6", "f4", "c4", "o2", "p7", "f5", "c5",
    "o3", "f6", "c6", "o4", "f7", "c7", "o5", "o6", "o7",
)


def kernel(
    act, ids, lengths, grads, weights, merged, mean_mass,
    piece, rows_t, act_t, windows, framed, fisher, own_w, got_w, own_mass, sent, got, blocks,
    a_send, a_recv, g_send, g_recv, z_send, z_recv, x_send, x_recv, w_send, w_recv, m_send, m_recv, own_sem,
):
    me = lax.axis_index("fsdp")
    y = lax.axis_index("ckpt")
    x, zc = me // 8, me % 8
    z, c = zc // 2, zc % 2
    up, down = (z + 1) % 4, (z + 3) % 4
    right, left = (x + 1) % 4, (x + 3) % 4
    offsets = [sum(CHUNKS[:j]) for j in range(len(CHUNKS))]
    n = len(CHUNKS)
    width = sum(CHUNKS)

    def plane(index):
        return {"fsdp": index, "ckpt": y}

    def column(index):
        return {"fsdp": me, "ckpt": index}

    barrier = pltpu.get_barrier_semaphore()

    @pl.loop(1, 32)
    def _(k):
        pl.semaphore_signal(barrier, inc=1, device_id=plane((me + k) % 32), device_id_type=MESH)

    for d in range(1, 4):
        pl.semaphore_signal(barrier, inc=1, device_id=column((y + d) % 4), device_id_type=MESH)
    pl.semaphore_wait(barrier, 34)

    def remote(src, dst, send, recv, target):
        return pltpu.make_async_remote_copy(
            src_ref=src, dst_ref=dst, send_sem=send, recv_sem=recv, device_id=target, device_id_type=MESH
        )

    def sized(ref, sem):
        pltpu.make_async_copy(ref, ref, sem).wait()

    def z_start(j):
        wide = CHUNKS[j]
        dst = blocks[j].at[me // 2, pl.ds(pl.multiple_of((me % 2) * 64, 64), 64)]

        def src(block):
            return grads.at[0, :, pl.ds(pl.multiple_of(block * width + offsets[j], 128), wide)]

        @pl.loop(1, 8)
        def _(k):
            other = (zc + k) % 8
            remote(src(other), dst, z_send.at[j], z_recv.at[j], plane(x * 8 + other)).start()

        pltpu.make_async_copy(src(zc), dst, z_recv.at[j]).start()

    def band(j, which, first=0, count=4):
        return blocks[j].at[pl.ds(which * 4 + first, count)]

    x_targets = {0: right, 1: left, 2: right, 3: left}

    def x_copy(j, i):
        part = (band(j, x), band(j, x), band(j, left, 0, 2), band(j, right, 2, 2))[i]
        return remote(part, part, x_send.at[j, i], x_recv.at[j, i], plane(x_targets[i] * 8 + zc))

    def x_arrived(j, i):
        part = (band(j, left), band(j, right), band(j, (x + 2) % 4, 0, 2), band(j, (x + 2) % 4, 2, 2))[i]
        sized(part, x_recv.at[j, i])

    def x_start(j):
        sized(band(j, x), z_recv.at[j])
        x_copy(j, 0).start()
        x_copy(j, 1).start()

    def x_pass(j):
        x_arrived(j, 0)
        x_copy(j, 2).start()
        x_arrived(j, 1)
        x_copy(j, 3).start()

    def x_finish(j):
        x_arrived(j, 2)
        x_arrived(j, 3)

    def a_source(target):
        return act.at[0, :, pl.ds(pl.multiple_of(target * 128, 128), 128)]

    a_rows = piece.at[pl.ds(pl.multiple_of(me * 64, 64), 64)]

    def a_start():
        @pl.loop(1, 32)
        def _(k):
            target = (me + k) % 32
            remote(a_source(target), a_rows, a_send, a_recv, plane(target)).start()

        pltpu.make_async_copy(a_source(me), a_rows, a_recv).start()

    def w_rows(owner):
        return weights.at[0, 0, pl.ds(pl.multiple_of(owner * 256, 256), 256)]

    w_copies = [
        remote(w_rows((y + d) % 4), got_w.at[d - 1], w_send.at[d - 1], w_recv.at[d - 1], column((y + d) % 4))
        for d in range(1, 4)
    ]
    own_copy = pltpu.make_async_copy(w_rows(y), own_w, own_sem)

    def w_start():
        for copy in w_copies:
            copy.start()
        own_copy.start()

    def w_arrived():
        own_copy.wait()
        for i in range(3):
            sized(got_w.at[i], w_recv.at[i])

    first_of = [jnp.int32(0)]
    for e in range(8):
        first_of.append(first_of[e] + lengths[0, e])

    lead, keeps = [], []
    for e in range(8):
        lead.append(jnp.minimum(first_of[e] // 128, 12))
        position = lead[e] * 128 + lax.broadcasted_iota(jnp.int32, (1, 512), 1)
        keep = (position >= first_of[e]) & (position < first_of[e] + lengths[0, e])
        keeps.append(jnp.where(keep, jnp.float32(1), jnp.float32(0)).astype(jnp.bfloat16))

    def a_turn():
        sized(piece, a_recv)

        @pl.loop(0, 8)
        def _(b):
            at = pl.ds(pl.multiple_of(b * 256, 256), 256)
            rows_t[:, at] = piece[at, :].astype(jnp.float32).T.astype(jnp.bfloat16)

    def hot_build():
        @pl.loop(0, 8)
        def _(b):
            own = ids[:, pl.ds(pl.multiple_of(b * 256, 256), 256)]
            for h in range(2):
                hot = lax.broadcasted_iota(jnp.int32, (1024, 256), 0) + h * 1024 == own
                hot = jnp.where(hot, jnp.float32(1), jnp.float32(0)).astype(jnp.bfloat16)
                windows[b, :, h * 256 : (h + 1) * 256] = hot

    def a_permute(half):
        @pl.loop(half * 4, half * 4 + 4)
        def _(b):
            placed = sum(
                jnp.dot(
                    rows_t[:, h * 1024 : (h + 1) * 1024],
                    windows[b, :, h * 256 : (h + 1) * 256],
                    preferred_element_type=jnp.float32,
                )
                for h in range(2)
            )
            for i in range(2):
                act_t[0][b * 2 + i] = placed[:, i * 128 : (i + 1) * 128].astype(jnp.bfloat16)

    above_core, below_core = plane(x * 8 + up * 2 + c), plane(x * 8 + down * 2 + c)
    other_core = plane(x * 8 + z * 2 + 1 - c)
    first_half, second_half = pl.ds(0, 8), pl.ds(8, 8)

    def g_copy(i):
        src, dst, target = (
            (act_t[0].at[first_half], act_t[1].at[first_half], above_core),
            (act_t[0].at[second_half], act_t[2].at[second_half], below_core),
            (act_t[1].at[first_half], act_t[3].at[first_half], above_core),
            (act_t[2].at[second_half], act_t[3].at[second_half], below_core),
            (act_t[0], act_t[4], other_core),
            (act_t[1], act_t[5], other_core),
            (act_t[2], act_t[6], other_core),
            (act_t[3], act_t[7], other_core),
            (act_t[0].at[second_half], act_t[1].at[second_half], above_core),
            (act_t[0].at[first_half], act_t[2].at[first_half], below_core),
        )[i]
        return remote(src, dst, g_send.at[i], g_recv.at[i], target)

    def g_arrived(i):
        part = (
            act_t[1].at[first_half], act_t[2].at[second_half], act_t[3].at[first_half], act_t[3].at[second_half],
            act_t[4], act_t[5], act_t[6], act_t[7],
            act_t[1].at[second_half], act_t[2].at[first_half],
        )[i]
        sized(part, g_recv.at[i])

    def mask(k):
        owner = (z + (0, 3, 1, 2)[k % 4]) % 4 * 2 + (c if k < 4 else 1 - c)
        for e in range(8):
            for i in range(4):
                at = slice(i * 128, (i + 1) * 128)
                rows = pl.ds(pl.multiple_of(owner * 128, 128), 128)
                windows[e, rows, at] = act_t[k][lead[e] + i] * keeps[e][:, at]

    def g_start():
        for i in (1, 8, 4):
            g_copy(i).start()

    def g_start_half():
        for i in (0, 9):
            g_copy(i).start()

    def g_below():
        g_arrived(0)
        g_copy(2).start()
        g_arrived(8)
        g_copy(5).start()

    def g_above():
        g_arrived(1)
        g_copy(3).start()
        g_arrived(9)
        g_copy(6).start()

    def g_far():
        g_arrived(2)
        g_arrived(3)
        g_copy(7).start()

    def mask_own():
        mask(0)
        g_arrived(4)
        mask(4)

    def mask_near():
        mask(1)
        mask(2)
        g_arrived(5)
        mask(5)
        g_arrived(6)
        mask(6)

    def mask_far():
        mask(3)
        g_arrived(7)
        mask(7)

    def m_copy(j, d):
        owner = (y + d) % 4
        return remote(
            sent[j].at[pl.ds(pl.multiple_of(owner * 256, 256), 256)],
            got[j].at[d - 1], m_send.at[j, d - 1], m_recv.at[j, d - 1], column(owner),
        )

    def rows_of(j, owner):
        wide = CHUNKS[j]
        at = pl.ds(pl.multiple_of(owner * 256, 256), 256)
        for e in range(8):
            part = jnp.dot(windows[e, at, :], framed[e, :, :wide], preferred_element_type=jnp.float32)
            part = part * part
            fisher[:, :wide] = part + (PRIOR if e == 0 else fisher[:, :wide])

        @pl.when(owner != y)
        def _():
            code = jnp.log(fisher[:, :wide]) * (SCALE / LN2) - (LOW * SCALE + 32767.5)
            code = jnp.clip(jnp.floor(code), -32768.0, 32767.0).astype(jnp.int32)
            sent[j][at, :] = code.astype(jnp.int16)
            m_copy(j, (owner + 4 - y) % 4).start()

        @pl.when(owner == y)
        def _():
            own_mass[:, offsets[j] : offsets[j] + wide] = fisher[:, :wide]

    def frame(j):
        for e in range(8):
            for i in range(4):
                framed[e, i * 128 : (i + 1) * 128, : CHUNKS[j]] = blocks[j][lead[e] + i]

    def compute(j):
        frame(j)

        @pl.loop(0, 4)
        def _(t):
            rows_of(j, (y + ((t + 1) % 3 + 1) * (1 - t // 3)) % 4)

    def combine(j):
        columns = slice(offsets[j], offsets[j] + CHUNKS[j])
        for d in range(1, 4):
            sized(got[j].at[d - 1], m_recv.at[j, d - 1])

        @pl.loop(0, 8)
        def _(q):
            at = pl.ds(pl.multiple_of(q * 32, 32), 32)
            total = own_mass[at, columns]
            weighted = total * own_w[at, columns].astype(jnp.float32)
            for d in range(3):
                code = got[j][d, at, :].astype(jnp.int32).astype(jnp.float32)
                mass = jnp.exp((code + (32768.0 + LOW * SCALE)) * (LN2 / SCALE))
                total += mass
                weighted += mass * got_w[d, at, columns].astype(jnp.float32)
            merged[0, at, columns] = (weighted / total).astype(jnp.bfloat16)
            mean_mass[0, at, columns] = total * 0.25

    steps = {
        "z": z_start, "s": x_start, "p": x_pass, "f": x_finish, "c": compute, "o": combine,
        "A": a_start, "W": w_start, "V": w_arrived, "T": a_turn, "H": hot_build, "P": a_permute, "G": g_start, "g": g_start_half, "B": g_below,
        "U": g_above, "F": g_far, "X": mask_own, "Y": mask_near, "Z": mask_far,
    }
    for step in ORDER:
        steps[step[0]](*(int(j) for j in step[1:]))

    pltpu.make_async_copy(piece.at[pl.ds(0, 31 * 64)], piece.at[pl.ds(0, 31 * 64)], a_send).wait()
    for copy in w_copies:
        copy.wait_send()
    for i in range(10):
        g_copy(i).wait_send()
    for j in range(n):
        sized(blocks[j].at[pl.ds(0, 7), pl.ds(0, 64)], z_send.at[j])
        for i in range(4):
            x_copy(j, i).wait_send()
        for d in range(1, 4):
            m_copy(j, d).wait_send()


def body(act_table, token_ids, lengths, grads, weights):
    n = len(CHUNKS)
    wide = sum(CHUNKS)
    dma = pltpu.SemaphoreType.DMA
    whole = pl.BlockSpec(memory_space=pltpu.VMEM)
    anywhere = pl.BlockSpec(memory_space=pl.ANY)
    operands = (act_table, token_ids, lengths, grads, weights)
    operands = [pltpu.with_memory_space_constraint(operand, pltpu.HBM) for operand in operands]
    return pl.pallas_call(
        kernel,
        out_shape=(
            jax.ShapeDtypeStruct((1, 256, wide), jnp.bfloat16),
            jax.ShapeDtypeStruct((1, 256, wide), jnp.float32),
        ),
        in_specs=[anywhere, whole, pl.BlockSpec(memory_space=pltpu.SMEM), anywhere, anywhere],
        out_specs=(whole, whole),
        scratch_shapes=[
            pltpu.VMEM((2048, 128), jnp.bfloat16),
            pltpu.VMEM((128, 2048), jnp.bfloat16),
            tuple(pltpu.VMEM((16, 128, 128), jnp.bfloat16) for _ in range(8)),
            pltpu.VMEM((8, 1024, 512), jnp.bfloat16),
            pltpu.VMEM((8, 512, max(CHUNKS)), jnp.bfloat16),
            pltpu.VMEM((256, max(CHUNKS)), jnp.float32),
            pltpu.VMEM((256, wide), jnp.bfloat16),
            pltpu.VMEM((3, 256, wide), jnp.bfloat16),
            pltpu.VMEM((256, wide), jnp.float32),
            tuple(pltpu.VMEM((1024, w), jnp.int16) for w in CHUNKS),
            tuple(pltpu.VMEM((3, 256, w), jnp.int16) for w in CHUNKS),
            tuple(pltpu.VMEM((16, 128, w), jnp.bfloat16) for w in CHUNKS),
            dma, dma, dma((10,)), dma((10,)), dma((n,)), dma((n,)), dma((n, 4)), dma((n, 4)),
            dma((3,)), dma((3,)), dma((n, 3)), dma((n, 3)), dma,
        ],
        compiler_params=pltpu.CompilerParams(
            collective_id=0, has_side_effects=True, vmem_limit_bytes=50 << 20
        ),
    )(*operands)


def solution(mesh):
    placed = (
        P("ckpt", "fsdp", None),
        P("ckpt", None),
        P("ckpt", None),
        P("ckpt", "fsdp", None),
        P("ckpt", "fsdp", None, None),
    )
    return jax.shard_map(
        body,
        mesh=mesh,
        in_specs=placed,
        out_specs=(P("fsdp", "ckpt", None), P("fsdp", "ckpt", None)),
        check_vma=False,
    )
```

```python
import jax
import jax.numpy as jnp
from jax import lax
from jax.experimental import pallas as pl
from jax.experimental.pallas import tpu as pltpu
from jax.sharding import PartitionSpec as P

PRIOR = 0.1
CHUNKS = (256,) * 6 + (128,) * 2
LOW, HIGH = -3.32195, 20.04
LN2 = 0.6931471805599453
SCALE = 65535.0 / (HIGH - LOW)
MESH = pl.DeviceIdType.MESH
ORDER = (
    "A", "z0", "z1", "H", "W", "z2", "s0", "s1", "T", "P0", "g", "P1", "G", "z3", "s2", "p0", "X", "B", "U", "z4",
    "s3", "p1", "F", "z5", "Y", "Z", "s4", "p2", "z6", "z7", "f0", "c0", "p3", "s5", "f1", "c1", "p4",
    "s6", "f2", "c2", "V", "o0", "p5", "s7", "f3", "c3", "o1", "p6", "f4", "c4", "o2", "p7", "f5", "c5",
    "o3", "f6", "c6", "o4", "f7", "c7", "o5", "o6", "o7",
)


def kernel(
    act, ids, lengths, grads, weights, merged, mean_mass,
    piece, rows_t, act_t, windows, framed, fisher, own_w, got_w, own_mass, sent, got, blocks,
    a_send, a_recv, g_send, g_recv, z_send, z_recv, x_send, x_recv, w_send, w_recv, m_send, m_recv, own_sem,
):
    me = lax.axis_index("fsdp")
    y = lax.axis_index("ckpt")
    x, zc = me // 8, me % 8
    z, c = zc // 2, zc % 2
    up, down = (z + 1) % 4, (z + 3) % 4
    right, left = (x + 1) % 4, (x + 3) % 4
    offsets = [sum(CHUNKS[:j]) for j in range(len(CHUNKS))]
    n = len(CHUNKS)
    width = sum(CHUNKS)

    def plane(index):
        return {"fsdp": index, "ckpt": y}

    def column(index):
        return {"fsdp": me, "ckpt": index}

    barrier = pltpu.get_barrier_semaphore()

    @pl.loop(1, 32)
    def _(k):
        pl.semaphore_signal(barrier, inc=1, device_id=plane((me + k) % 32), device_id_type=MESH)

    for d in range(1, 4):
        pl.semaphore_signal(barrier, inc=1, device_id=column((y + d) % 4), device_id_type=MESH)
    pl.semaphore_wait(barrier, 34)

    def remote(src, dst, send, recv, target):
        return pltpu.make_async_remote_copy(
            src_ref=src, dst_ref=dst, send_sem=send, recv_sem=recv, device_id=target, device_id_type=MESH
        )

    def sized(ref, sem):
        pltpu.make_async_copy(ref, ref, sem).wait()

    def z_start(j):
        wide = CHUNKS[j]
        dst = blocks[j].at[me // 2, pl.ds(pl.multiple_of((me % 2) * 64, 64), 64)]

        def src(block):
            return grads.at[0, :, pl.ds(pl.multiple_of(block * width + offsets[j], 128), wide)]

        @pl.loop(1, 8)
        def _(k):
            other = (zc + k) % 8
            remote(src(other), dst, z_send.at[j], z_recv.at[j], plane(x * 8 + other)).start()

        pltpu.make_async_copy(src(zc), dst, z_recv.at[j]).start()

    def band(j, which, first=0, count=4):
        return blocks[j].at[pl.ds(which * 4 + first, count)]

    x_targets = {0: right, 1: left, 2: right, 3: left}

    def x_copy(j, i):
        part = (band(j, x), band(j, x), band(j, left, 0, 2), band(j, right, 2, 2))[i]
        return remote(part, part, x_send.at[j, i], x_recv.at[j, i], plane(x_targets[i] * 8 + zc))

    def x_arrived(j, i):
        part = (band(j, left), band(j, right), band(j, (x + 2) % 4, 0, 2), band(j, (x + 2) % 4, 2, 2))[i]
        sized(part, x_recv.at[j, i])

    def x_start(j):
        sized(band(j, x), z_recv.at[j])
        x_copy(j, 0).start()
        x_copy(j, 1).start()

    def x_pass(j):
        x_arrived(j, 0)
        x_copy(j, 2).start()
        x_arrived(j, 1)
        x_copy(j, 3).start()

    def x_finish(j):
        x_arrived(j, 2)
        x_arrived(j, 3)

    def a_source(target):
        return act.at[0, :, pl.ds(pl.multiple_of(target * 128, 128), 128)]

    a_rows = piece.at[pl.ds(pl.multiple_of(me * 64, 64), 64)]

    def a_start():
        @pl.loop(1, 32)
        def _(k):
            target = (me + k) % 32
            remote(a_source(target), a_rows, a_send, a_recv, plane(target)).start()

        pltpu.make_async_copy(a_source(me), a_rows, a_recv).start()

    def w_rows(owner):
        return weights.at[0, 0, pl.ds(pl.multiple_of(owner * 256, 256), 256)]

    w_copies = [
        remote(w_rows((y + d) % 4), got_w.at[d - 1], w_send.at[d - 1], w_recv.at[d - 1], column((y + d) % 4))
        for d in range(1, 4)
    ]
    own_copy = pltpu.make_async_copy(w_rows(y), own_w, own_sem)

    def w_start():
        for copy in w_copies:
            copy.start()
        own_copy.start()

    def w_arrived():
        own_copy.wait()
        for i in range(3):
            sized(got_w.at[i], w_recv.at[i])

    first_of = [jnp.int32(0)]
    for e in range(8):
        first_of.append(first_of[e] + lengths[0, e])

    lead, keeps = [], []
    for e in range(8):
        lead.append(jnp.minimum(first_of[e] // 128, 12))
        position = lead[e] * 128 + lax.broadcasted_iota(jnp.int32, (1, 512), 1)
        keep = (position >= first_of[e]) & (position < first_of[e] + lengths[0, e])
        keeps.append(jnp.where(keep, jnp.float32(1), jnp.float32(0)).astype(jnp.bfloat16))

    def a_turn():
        sized(piece, a_recv)

        @pl.loop(0, 8)
        def _(b):
            at = pl.ds(pl.multiple_of(b * 256, 256), 256)
            rows_t[:, at] = piece[at, :].astype(jnp.float32).T.astype(jnp.bfloat16)

    def hot_build():
        @pl.loop(0, 8)
        def _(b):
            own = ids[:, pl.ds(pl.multiple_of(b * 256, 256), 256)]
            for h in range(2):
                hot = lax.broadcasted_iota(jnp.int32, (1024, 256), 0) + h * 1024 == own
                hot = jnp.where(hot, jnp.float32(1), jnp.float32(0)).astype(jnp.bfloat16)
                windows[b, :, h * 256 : (h + 1) * 256] = hot

    def a_permute(half):
        @pl.loop(half * 4, half * 4 + 4)
        def _(b):
            placed = sum(
                jnp.dot(
                    rows_t[:, h * 1024 : (h + 1) * 1024],
                    windows[b, :, h * 256 : (h + 1) * 256],
                    preferred_element_type=jnp.float32,
                )
                for h in range(2)
            )
            for i in range(2):
                act_t[0][b * 2 + i] = placed[:, i * 128 : (i + 1) * 128].astype(jnp.bfloat16)

    above_core, below_core = plane(x * 8 + up * 2 + c), plane(x * 8 + down * 2 + c)
    other_core = plane(x * 8 + z * 2 + 1 - c)
    first_half, second_half = pl.ds(0, 8), pl.ds(8, 8)

    def g_copy(i):
        src, dst, target = (
            (act_t[0].at[first_half], act_t[1].at[first_half], above_core),
            (act_t[0].at[second_half], act_t[2].at[second_half], below_core),
            (act_t[1].at[first_half], act_t[3].at[first_half], above_core),
            (act_t[2].at[second_half], act_t[3].at[second_half], below_core),
            (act_t[0], act_t[4], other_core),
            (act_t[1], act_t[5], other_core),
            (act_t[2], act_t[6], other_core),
            (act_t[3], act_t[7], other_core),
            (act_t[0].at[second_half], act_t[1].at[second_half], above_core),
            (act_t[0].at[first_half], act_t[2].at[first_half], below_core),
        )[i]
        return remote(src, dst, g_send.at[i], g_recv.at[i], target)

    def g_arrived(i):
        part = (
            act_t[1].at[first_half], act_t[2].at[second_half], act_t[3].at[first_half], act_t[3].at[second_half],
            act_t[4], act_t[5], act_t[6], act_t[7],
            act_t[1].at[second_half], act_t[2].at[first_half],
        )[i]
        sized(part, g_recv.at[i])

    def mask(k):
        owner = (z + (0, 3, 1, 2)[k % 4]) % 4 * 2 + (c if k < 4 else 1 - c)
        for e in range(8):
            for i in range(4):
                at = slice(i * 128, (i + 1) * 128)
                rows = pl.ds(pl.multiple_of(owner * 128, 128), 128)
                windows[e, rows, at] = act_t[k][lead[e] + i] * keeps[e][:, at]

    def g_start():
        for i in (1, 8, 4):
            g_copy(i).start()

    def g_start_half():
        for i in (0, 9):
            g_copy(i).start()

    def g_below():
        g_arrived(0)
        g_copy(2).start()
        g_arrived(8)
        g_copy(5).start()

    def g_above():
        g_arrived(1)
        g_copy(3).start()
        g_arrived(9)
        g_copy(6).start()

    def g_far():
        g_arrived(2)
        g_arrived(3)
        g_copy(7).start()

    def mask_own():
        mask(0)
        g_arrived(4)
        mask(4)

    def mask_near():
        mask(1)
        mask(2)
        g_arrived(5)
        mask(5)
        g_arrived(6)
        mask(6)

    def mask_far():
        mask(3)
        g_arrived(7)
        mask(7)

    def m_copy(j, d):
        owner = (y + d) % 4
        return remote(
            sent[j].at[pl.ds(pl.multiple_of(owner * 256, 256), 256)],
            got[j].at[d - 1], m_send.at[j, d - 1], m_recv.at[j, d - 1], column(owner),
        )

    def rows_of(j, owner):
        wide = CHUNKS[j]
        at = pl.ds(pl.multiple_of(owner * 256, 256), 256)
        for e in range(8):
            part = jnp.dot(windows[e, at, :], framed[e, :, :wide], preferred_element_type=jnp.float32)
            part = part * part
            fisher[:, :wide] = part + (PRIOR if e == 0 else fisher[:, :wide])

        @pl.when(owner != y)
        def _():
            code = jnp.log(fisher[:, :wide]) * (SCALE / LN2) - (LOW * SCALE + 32767.5)
            code = jnp.clip(jnp.floor(code), -32768.0, 32767.0).astype(jnp.int32)
            sent[j][at, :] = code.astype(jnp.int16)
            m_copy(j, (owner + 4 - y) % 4).start()

        @pl.when(owner == y)
        def _():
            own_mass[:, offsets[j] : offsets[j] + wide] = fisher[:, :wide]

    def frame(j):
        for e in range(8):
            for i in range(4):
                framed[e, i * 128 : (i + 1) * 128, : CHUNKS[j]] = blocks[j][lead[e] + i]

    def compute(j):
        frame(j)

        @pl.loop(0, 4)
        def _(t):
            rows_of(j, (y + ((t + 1) % 3 + 1) * (1 - t // 3)) % 4)

    def combine(j):
        columns = slice(offsets[j], offsets[j] + CHUNKS[j])
        for d in range(1, 4):
            sized(got[j].at[d - 1], m_recv.at[j, d - 1])

        @pl.loop(0, 8)
        def _(q):
            at = pl.ds(pl.multiple_of(q * 32, 32), 32)
            total = own_mass[at, columns]
            weighted = total * own_w[at, columns].astype(jnp.float32)
            for d in range(3):
                code = got[j][d, at, :].astype(jnp.int32).astype(jnp.float32)
                mass = jnp.exp((code + (32768.0 + LOW * SCALE)) * (LN2 / SCALE))
                total += mass
                weighted += mass * got_w[d, at, columns].astype(jnp.float32)
            merged[0, at, columns] = (weighted / total).astype(jnp.bfloat16)
            mean_mass[0, at, columns] = total * 0.25

    steps = {
        "z": z_start, "s": x_start, "p": x_pass, "f": x_finish, "c": compute, "o": combine,
        "A": a_start, "W": w_start, "V": w_arrived, "T": a_turn, "H": hot_build, "P": a_permute, "G": g_start, "g": g_start_half, "B": g_below,
        "U": g_above, "F": g_far, "X": mask_own, "Y": mask_near, "Z": mask_far,
    }
    for step in ORDER:
        steps[step[0]](*(int(j) for j in step[1:]))

    pltpu.make_async_copy(piece.at[pl.ds(0, 31 * 64)], piece.at[pl.ds(0, 31 * 64)], a_send).wait()
    for copy in w_copies:
        copy.wait_send()
    for i in range(10):
        g_copy(i).wait_send()
    for j in range(n):
        sized(blocks[j].at[pl.ds(0, 7), pl.ds(0, 64)], z_send.at[j])
        for i in range(4):
            x_copy(j, i).wait_send()
        for d in range(1, 4):
            m_copy(j, d).wait_send()


def body(act_table, token_ids, lengths, grads, weights):
    n = len(CHUNKS)
    wide = sum(CHUNKS)
    dma = pltpu.SemaphoreType.DMA
    whole = pl.BlockSpec(memory_space=pltpu.VMEM)
    anywhere = pl.BlockSpec(memory_space=pl.ANY)
    operands = (act_table, token_ids, lengths, grads, weights)
    operands = [pltpu.with_memory_space_constraint(operand, pltpu.HBM) for operand in operands]
    return pl.pallas_call(
        kernel,
        out_shape=(
            jax.ShapeDtypeStruct((1, 256, wide), jnp.bfloat16),
            jax.ShapeDtypeStruct((1, 256, wide), jnp.float32),
        ),
        in_specs=[anywhere, whole, pl.BlockSpec(memory_space=pltpu.SMEM), anywhere, anywhere],
        out_specs=(whole, whole),
        scratch_shapes=[
            pltpu.VMEM((2048, 128), jnp.bfloat16),
            pltpu.VMEM((128, 2048), jnp.bfloat16),
            tuple(pltpu.VMEM((16, 128, 128), jnp.bfloat16) for _ in range(8)),
            pltpu.VMEM((8, 1024, 512), jnp.bfloat16),
            pltpu.VMEM((8, 512, max(CHUNKS)), jnp.bfloat16),
            pltpu.VMEM((256, max(CHUNKS)), jnp.float32),
            pltpu.VMEM((256, wide), jnp.bfloat16),
            pltpu.VMEM((3, 256, wide), jnp.bfloat16),
            pltpu.VMEM((256, wide), jnp.float32),
            tuple(pltpu.VMEM((1024, w), jnp.int16) for w in CHUNKS),
            tuple(pltpu.VMEM((3, 256, w), jnp.int16) for w in CHUNKS),
            tuple(pltpu.VMEM((16, 128, w), jnp.bfloat16) for w in CHUNKS),
            dma, dma, dma((10,)), dma((10,)), dma((n,)), dma((n,)), dma((n, 4)), dma((n, 4)),
            dma((3,)), dma((3,)), dma((n, 3)), dma((n, 3)), dma,
        ],
        compiler_params=pltpu.CompilerParams(
            collective_id=0, has_side_effects=True, vmem_limit_bytes=50 << 20
        ),
    )(*operands)


def solution(mesh):
    placed = (
        P("ckpt", "fsdp", None),
        P("ckpt", None),
        P("ckpt", None),
        P("ckpt", "fsdp", None),
        P("ckpt", "fsdp", None, None),
    )
    return jax.shard_map(
        body,
        mesh=mesh,
        in_specs=placed,
        out_specs=(P("fsdp", "ckpt", None), P("fsdp", "ckpt", None)),
        check_vma=False,
    )
```
